32 devices in a mesh: groups: 2 (over y), fsdp: 8 (over z, x), tensor: 2 (over core).
Axes of the slice: x: 2, y: 2, z: 4, core: 2. Of those that a mesh axis runs over, the one named last changes fastest.
Arguments:
- token_ids: int32 [4, 64], P(None, 'groups'), parts along dimension 1, may hold values from 0 to 76031
- embed_table: bfloat16 [5120, 76032], P(('fsdp', 'tensor')), may hold values from -9 to 9
- norm_gain: bfloat16 [5120], replicated, may hold values from 0.099609375 to 1.8984375
- gate_base: bfloat16 [12800, 5120], P(('fsdp', 'tensor')), may hold values from -0.078125 to 0.078125
- up_base: bfloat16 [12800, 5120], P(('fsdp', 'tensor')), may hold values from -0.078125 to 0.078125
- down_base: bfloat16 [12800, 5120], P(('fsdp', 'tensor')), may hold values from -0.078125 to 0.078125
- gate_up_b: bfloat16 [5120, 128], P('fsdp'), may hold values from -0.078125 to 0.078125
- gate_up_a: bfloat16 [128, 12800], P(None, 'fsdp'), may hold values from -0.75 to 0.75
- down_b: bfloat16 [12800, 64], P('fsdp'), may hold values from -0.0546875 to 0.0546875
- down_a: bfloat16 [64, 5120], P(None, 'fsdp'), may hold values from -0.75 to 0.75
Outputs:
- final_stream: bfloat16 [64, 5120], P('groups', ('fsdp', 'tensor')), parts along dimension 0
The draws below stay inside these ranges and needn't reach their ends.
There are 2 independent parts, one for each index of `groups`. The reference program is written for one: setup_inputs(seed, part) draws one part's arguments, and reference() takes and returns one part's arrays. A program takes and returns all parts, laid end to end along the dimension named above; an argument that names none is the same for every part. Nothing has to cross between parts.
All inputs are finite; a program needn't handle non-finite values.
Results may differ from the reference program's by a relative error of at most 0.012.
Values may be sent and summed in bfloat16 or wider, within the bound.
A program may use at most 256 MiB of HBM per device.

```python
import math
import jax
import jax.numpy as jnp
import numpy as np
from jax import lax

D = 5120
FF = 12800
RANK = 64
VOCAB = 76032
STEPS = 4
ROWS = 32


def draw_embed_table(key, part):
    key = jax.random.fold_in(key, 11)
    column_pos = jnp.arange(D, dtype=jnp.float32) / D
    values = jnp.clip(jax.random.normal(key, (D, VOCAB), jnp.float32), -6.0, 6.0)
    scales = 0.5 + column_pos
    return (values * scales[:, None]).astype(jnp.bfloat16)


def plant(result, key, smallest, largest):
    dims = result.shape
    place = [jax.random.randint(jax.random.fold_in(key, axis), (), 0, dims[axis]) for axis in range(len(dims))]
    result = result.at[tuple(place)].set(smallest)
    longest = dims.index(max(dims))
    place[longest] = (place[longest] + 1) % dims[longest]
    return result.at[tuple(place)].set(largest)


def with_spikes(drawn, own_key, source, target, parts, factor):
    def block_of(axis_at):
        return (jnp.arange(drawn.shape[axis_at]) // (drawn.shape[axis_at] // parts)).reshape((-1,) + (1,) * (drawn.ndim - 1 - axis_at))

    first = jax.random.permutation(own_key, parts)[block_of(target)]
    far = (block_of(target) + parts // 2) % parts
    return jnp.where((block_of(source) == first) | (block_of(source) == far), factor * drawn, drawn)


def steps_of(key, dims, split, smallest, largest):
    factor_of, own = 1.0, jax.random.fold_in(key, 6)
    for dim, parts in split:
        steps = jnp.exp(jax.random.uniform(jax.random.fold_in(own, dim), (parts,), jnp.float32, smallest / len(split), largest / len(split)))
        factor_of = factor_of * jnp.repeat(steps, dims[dim] // parts).reshape([-1 if axis == dim else 1 for axis in range(len(dims))])
    return factor_of


def wide_ids(key, dims, number_of, slope):
    weights = [min(1 << octave, number_of + 1 - (1 << octave)) * (1 << 20) // math.isqrt((1 << octave) ** slope) + 1 for octave in range((number_of + 1).bit_length()) if 1 << octave <= number_of]
    width = 1 + sum(weights) // (1 << 30)
    table = np.cumsum(np.array([max(1, weight // width) for weight in weights]))
    ticket = jax.random.randint(jax.random.fold_in(key, 1), dims, 0, int(table[len(weights) - 1]))
    start = jnp.left_shift(1, jnp.searchsorted(jnp.asarray(table, jnp.int32), ticket, side="right").astype(jnp.int32))
    standing = start - 1 + jax.random.randint(jax.random.fold_in(key, 4), dims, 0, 1 << 30) % jnp.minimum(start, number_of + 1 - start)
    return jax.random.permutation(jax.random.fold_in(key, 2), number_of)[standing].astype(jnp.int32)


def noise(rng, shape, deviation, reach, shards=(), held_as=jnp.bfloat16):
    drawn = jax.random.normal(rng, shape, jnp.float32) * deviation
    if len(shards) > 0:
        drawn = steps_of(rng, shape, shards, -0.22, 0.18) * drawn
    return jnp.clip(drawn, min=-reach, max=reach).astype(held_as)


def bell_draw_with(key, shape, width, most, shards, heavy, kind=jnp.bfloat16):
    entries = width * jax.random.normal(key, shape, jnp.float32)
    if shards:
        entries = entries * steps_of(key, shape, shards, -0.22, 0.18)
    return jnp.clip(with_spikes(entries, jax.random.fold_in(key, 3), *heavy), -most, most).astype(kind)


def setup_inputs(seed: int = 0, part: int = 0) -> dict:
    streams_of = jax.random.split(jax.random.key(seed), 11)
    part_keys = jax.random.split(jax.random.fold_in(streams_of[10], part), 11)
    return {
        "token_ids": plant(wide_ids(part_keys[0], (STEPS, ROWS), VOCAB, 2), jax.random.fold_in(part_keys[0], 3), 0, VOCAB - 1).astype(jnp.int32),
        "embed_table": draw_embed_table(jax.random.fold_in(streams_of[10], 71), part),
        "norm_gain": jnp.clip(1.0 + 0.18 * jax.random.normal(streams_of[2], (D,), jnp.float32), 0.099609375, 1.8984375).astype(jnp.bfloat16),
        "gate_base": noise(streams_of[3], (FF, D), D ** -0.5, 0.078125, ((0, 16),)),
        "up_base": noise(streams_of[4], (FF, D), D ** -0.5, 0.078125, ((0, 16),)),
        "down_base": bell_draw_with(streams_of[5], (FF, D), FF ** -0.5, 0.078125, ((0, 16),), (0, 1, 16, 2.0)),
        "gate_up_b": noise(streams_of[6], (D, 2 * RANK), D ** -0.5, 0.078125, ((0, 8),)),
        "gate_up_a": noise(streams_of[7], (2 * RANK, FF), RANK ** -0.5, 0.75, ((1, 8),)),
        "down_b": noise(streams_of[8], (FF, RANK), FF ** -0.5, 0.0546875, ((0, 8),)),
        "down_a": noise(streams_of[9], (RANK, D), RANK ** -0.5, 0.75, ((1, 8),)),
    }


epsilon = 1e-06

def reference(token_ids, embed_table, norm_gain, gate_base, up_base, down_base, gate_up_b, gate_up_a, down_b, down_a):
    gate_w = (gate_base.astype(jnp.float32) + jnp.dot(gate_up_a[:RANK].T, gate_up_b[:, :RANK].T, preferred_element_type=jnp.float32)).astype(jnp.bfloat16)
    up_w = (up_base.astype(jnp.float32) + jnp.dot(gate_up_a[RANK:].T, gate_up_b[:, RANK:].T, preferred_element_type=jnp.float32)).astype(jnp.bfloat16)
    down_w = (down_base.astype(jnp.float32) + jnp.dot(down_b, down_a, preferred_element_type=jnp.float32)).astype(jnp.bfloat16)
    looked = jnp.transpose(jnp.take(embed_table, token_ids, axis=1), (1, 2, 0))
    gain_value = norm_gain.astype(jnp.float32)
    stream = jnp.zeros((ROWS, D), jnp.float32)
    for position in range(STEPS):
        stream = stream + looked[position].astype(jnp.float32)
        inverse_rms = lax.rsqrt(lax.optimization_barrier(jnp.mean(stream * stream, axis=1, keepdims=True)) + epsilon)
        normed = (stream * inverse_rms * gain_value).astype(jnp.bfloat16)
        gate_value = jnp.dot(normed, gate_w.T, preferred_element_type=jnp.float32)
        up_value = jnp.dot(normed, up_w.T, preferred_element_type=jnp.float32)
        activated = (jax.nn.silu(gate_value) * up_value).astype(jnp.bfloat16)
        stream = stream + jnp.dot(activated, down_w, preferred_element_type=jnp.float32)
    return stream.astype(jnp.bfloat16)
```

```python
import functools
import jax
import jax.numpy as jnp
from jax import lax
from jax.experimental import pallas as pl
from jax.experimental.pallas import tpu as pltpu
from jax.sharding import PartitionSpec as P

epsilon = 1e-06
bf16, f32 = jnp.bfloat16, jnp.float32
NT = (((1,), (1,)), ((), ()))
MESH = pl.DeviceIdType.MESH


def gather_kernel(ids_ref, table_ref, out_ref, blocks, placed, sems):
    count = blocks.shape[0]
    rows = table_ref.shape[0]

    def block_copy(i):
        start = pl.multiple_of((ids_ref[i] // 128) * 128, 128)
        return pltpu.make_async_copy(
            table_ref.at[:, pl.ds(start, 128)], blocks.at[i], sems.at[i]
        )

    def begin(i, carry):
        block_copy(i).start()
        return carry

    lax.fori_loop(0, count, begin, 0)
    placed[...] = jnp.zeros_like(placed)
    lane = lax.broadcasted_iota(jnp.int32, (rows, 128), 1)

    def place(i, carry):
        block_copy(i).wait()
        shift = lax.rem(i + 128 - lax.rem(ids_ref[i], 128), 128)
        turned = pltpu.roll(blocks[i].astype(f32), shift, 1)
        placed[:rows, :] = jnp.where(lane == i, turned, placed[:rows, :])
        return carry

    lax.fori_loop(0, count, place, 0)
    out = jnp.transpose(placed[...])[:, :rows].astype(bf16)
    out_ref[...] = out.reshape(out_ref.shape)


def gather_columns(token_ids, table):
    steps, rows = token_ids.shape
    count = steps * rows
    width = table.shape[0]
    padded = (width + 127) // 128 * 128
    return pl.pallas_call(
        gather_kernel,
        out_shape=jax.ShapeDtypeStruct((steps, 2, rows // 2, width), bf16),
        in_specs=[
            pl.BlockSpec(memory_space=pltpu.SMEM),
            pl.BlockSpec(memory_space=pl.ANY),
        ],
        out_specs=pl.BlockSpec(memory_space=pltpu.VMEM),
        scratch_shapes=[
            pltpu.VMEM((count, width, 128), bf16),
            pltpu.VMEM((padded, 128), f32),
            pltpu.SemaphoreType.DMA((count,)),
        ],
        compiler_params=pltpu.CompilerParams(vmem_limit_bytes=24 << 20),
        cost_estimate=pl.CostEstimate(
            flops=count * width * 128, bytes_accessed=count * width * 256, transcendentals=0
        ),
        name="embed_columns",
    )(token_ids.reshape(count), table)


def decode_kernel(
    F, X, looked_ref, gain_ref, gub_ref, gua_ref, dbt_ref, da_ref, gate_hbm, up_hbm, down_hbm,
    out_ref,
    wg, wu, wd, db, ag, stream, added, looked_in, acc_g, acc_u, act,
    sib_out, sib_in, own_part, rs_out, rs_in, fin_out, fin_in,
    w_sem, look_sem, ag_send, ag_recv, fw_send, fw_recv, sib_send, sib_recv, rs_send, rs_recv,
    fin_sem,
):
    S = looked_ref.shape[0]
    H = wg.shape[1]
    C = wg.shape[2]
    half = C // 2
    R = da_ref.shape[0]
    rows = 32
    Z = F // X
    grp = lax.axis_index("groups")
    me = lax.axis_index("fsdp")
    t = lax.axis_index("tensor")
    other = 1 - t
    z, x = me // X, me % X

    def ahead(k):
        return ((z + k // X) % Z) * X + (x + k % X) % X

    def behind(k):
        return ((z + Z - k // X) % Z) * X + (x + X - k % X) % X

    def w_copies(j, i):
        cols = pl.ds(pl.multiple_of(j * C, 128), C)
        return [
            pltpu.make_async_copy(h.at[:, cols], w.at[j], w_sem.at[n, i])
            for n, (h, w) in enumerate(((gate_hbm, wg), (up_hbm, wu), (down_hbm, wd)))
        ]

    for k in range(F):
        for c in w_copies(behind(k), k)[:2]:
            c.start()
    for i, k in enumerate(list(range(1, F)) + [0]):
        w_copies(ahead(k), i)[2].start()

    barrier = pltpu.get_barrier_semaphore()
    for k in range(1, F):
        pl.semaphore_signal(barrier, inc=1, device_id=(grp, ahead(k), t), device_id_type=MESH)
    pl.semaphore_signal(barrier, inc=1, device_id=(grp, me, other), device_id_type=MESH)
    pl.semaphore_wait(barrier, F)

    def remote(src, dst, ss, rs, dev):
        return pltpu.make_async_remote_copy(
            src_ref=src, dst_ref=dst, send_sem=ss, recv_sem=rs, device_id=dev, device_id_type=MESH
        )

    sibling = (grp, me, other)
    look = remote(looked_ref.at[:, other], looked_in, look_sem.at[0], look_sem.at[1], sibling)
    look.start()
    wide = dbt_ref[...]
    db[...] = jnp.where(t == 0, wide[:, :H].astype(f32), wide[:, H:].astype(f32)).astype(bf16)
    mine = looked_ref[:, t].astype(f32)
    look.wait()
    theirs = looked_in[...].astype(f32)
    for s in range(S):
        left = jnp.where(t == 0, mine[s], theirs[s])
        right = jnp.where(t == 0, theirs[s], mine[s])
        added[s] = jnp.concatenate([left, right], axis=1)
    stream[...] = jnp.zeros_like(stream)
    lane = lax.broadcasted_iota(jnp.int32, (rows, 2 * R), 1)

    def step(s, carry):
        now = stream[...] + added[s]
        stream[...] = now
        scaled = (now * gain_ref[pl.ds(me, 1), :]).astype(bf16)
        low = jnp.dot(scaled, gub_ref[...], preferred_element_type=f32)
        ag[s, me, t, :, :C] = now.astype(bf16)
        ag[s, me, t, :, C:] = low.astype(bf16)

        def ag_copy(j_from, k, dev):
            piece = ag.at[s, j_from, t]
            return remote(piece, piece, ag_send.at[k], ag_recv.at[s, j_from], dev)

        def fw_copy(j_from, k):
            piece = ag.at[s, j_from, t]
            return remote(piece, piece, fw_send.at[k], fw_recv.at[s, j_from], sibling)

        fw_copy(me, 0).start()
        for k in range(1, F):
            ag_copy(me, k, (grp, ahead(k), t)).start()

        squares = jnp.zeros((rows, 1), f32)
        lows = jnp.zeros((rows, 2 * R), f32)
        for k in range(F):
            if k + 1 < F:
                j_next = behind(k + 1)
                ag_copy(j_next, k + 1, (grp, j_next, t)).wait_recv()
                fw_copy(j_next, k + 1).start()
            j = behind(k)
            theirs_in = ag.at[s, j, other]
            remote(
                theirs_in, theirs_in, fw_send.at[k], fw_recv.at[s, j], sibling
            ).wait_recv()

            @pl.when(s == 0)
            def _():
                for c in w_copies(j, k)[:2]:
                    c.wait()

            piece = ag[s, j].reshape(rows, C + 2 * R)
            xs = piece[:, :C].astype(f32)
            squares += jnp.sum(xs * xs, axis=1, keepdims=True)
            lows += piece[:, C:].astype(f32)
            xn = (xs * gain_ref[pl.ds(j, 1), :]).astype(bf16)
            g = lax.dot_general(xn, wg[j], NT, preferred_element_type=f32)
            u = lax.dot_general(xn, wu[j], NT, preferred_element_type=f32)
            if k == 0:
                acc_g[...] = g
                acc_u[...] = u
            else:
                acc_g[...] += g
                acc_u[...] += u
        for k in range(1, F):
            ag_copy(me, k, (grp, ahead(k), t)).wait_send()
        for k in range(F):
            fw_copy(behind(k), k).wait_send()

        inverse_rms = lax.rsqrt(squares / (F * C) + epsilon)
        a_local = gua_ref[pl.ds(pl.multiple_of(t * H, 16), H), :]
        zero = jnp.zeros_like(lows)
        low_g = jnp.where(lane < R, lows, zero).astype(bf16)
        low_u = jnp.where(lane < R, zero, lows).astype(bf16)
        gate = acc_g[...] + lax.dot_general(low_g, a_local, NT, preferred_element_type=f32)
        up = acc_u[...] + lax.dot_general(low_u, a_local, NT, preferred_element_type=f32)
        gate = gate * inverse_rms
        up = up * inverse_rms
        act[...] = (gate / (1.0 + jnp.exp(-gate)) * up).astype(bf16)

        down_low = lax.dot_general(act[...], db[...], NT, preferred_element_type=f32)
        low_mine = jnp.where(t == 0, down_low[:16], down_low[16:])
        low_other = jnp.where(t == 0, down_low[16:], down_low[:16]).astype(bf16)

        def sib_copy(j):
            return remote(
                sib_out.at[j], sib_in.at[s, j], sib_send.at[j], sib_recv.at[s, j], sibling
            )

        def rs_copy(k):
            j = ahead(k)
            return remote(
                rs_out.at[j], rs_in.at[s, me], rs_send.at[k], rs_recv.at[s, me], (grp, j, t)
            )

        def finish(k):
            j = ahead(k)
            sib_copy(j).wait_recv()
            total = own_part[j] + sib_in[s, j].astype(f32)
            if k > 0:
                rs_out[j] = total.astype(bf16)
                rs_copy(k).start()
            return total

        order = list(range(1, F)) + [0]
        total = None
        for i, k in enumerate(order):
            j = ahead(k)

            @pl.when(s == 0)
            def _():
                w_copies(j, i)[2].wait()

            part = jnp.dot(act[...], wd[j], preferred_element_type=f32)
            own_part[j, :, :C] = jnp.where(t == 0, part[:16], part[16:])
            own_part[j, :, C:] = low_mine
            sib_out[j, :, :C] = jnp.where(t == 0, part[16:], part[:16]).astype(bf16)
            sib_out[j, :, C:] = low_other
            sib_copy(j).start()
            if i > 0:
                finish(order[i - 1])
        total = finish(0)
        for k in range(1, F):
            j = behind(k)
            remote(
                rs_out.at[j], rs_in.at[s, j], rs_send.at[k], rs_recv.at[s, j], (grp, j, t)
            ).wait_recv()
            total += rs_in[s, j].astype(f32)
        fix = jnp.dot(total[:, C:C + R].astype(bf16), da_ref[...], preferred_element_type=f32)
        stream[...] = stream[...] + total[:, :C] + fix
        for k in range(F):
            sib_copy(ahead(k)).wait_send()
            if k > 0:
                rs_copy(k).wait_send()
        return carry

    lax.fori_loop(0, S, step, 0)

    last = stream[...]
    keep = jnp.where(t == 0, last[:, :half], last[:, half:])
    fin_out[...] = jnp.where(t == 0, last[:, half:], last[:, :half]).astype(bf16)
    fin = remote(fin_out, fin_in, fin_sem.at[0], fin_sem.at[1], sibling)
    fin.start()
    out_ref[t] = keep.astype(bf16)
    fin.wait()
    out_ref[other] = fin_in[...]


def decode_steps(F, X, looked, gain, gub, gua_t, dbt, da, gate_base, up_base, down_base):
    S = looked.shape[0]
    H, D = gate_base.shape
    C = D // F
    R = da.shape[0]
    W = C + 2 * R
    vmem = pl.BlockSpec(memory_space=pltpu.VMEM)
    hbm = pl.BlockSpec(memory_space=pl.ANY)
    dma = pltpu.SemaphoreType.DMA
    return pl.pallas_call(
        functools.partial(decode_kernel, F, X),
        out_shape=jax.ShapeDtypeStruct((2, 16, C // 2), bf16),
        in_specs=[vmem] * 6 + [hbm] * 3,
        out_specs=vmem,
        scratch_shapes=[
            pltpu.VMEM((F, H, C), bf16),
            pltpu.VMEM((F, H, C), bf16),
            pltpu.VMEM((F, H, C), bf16),
            pltpu.VMEM((2 * R, H), bf16),
            pltpu.VMEM((S, F, 2, 16, W), bf16),
            pltpu.VMEM((16, C), f32),
            pltpu.VMEM((S, 16, C), f32),
            pltpu.VMEM((S, 16, C // 2), bf16),
            pltpu.VMEM((32, H), f32),
            pltpu.VMEM((32, H), f32),
            pltpu.VMEM((32, H), bf16),
            pltpu.VMEM((F, 16, W), bf16),
            pltpu.VMEM((S, F, 16, W), bf16),
            pltpu.VMEM((F, 16, W), f32),
            pltpu.VMEM((F, 16, W), bf16),
            pltpu.VMEM((S, F, 16, W), bf16),
            pltpu.VMEM((16, C // 2), bf16),
            pltpu.VMEM((16, C // 2), bf16),
            dma((3, F)),
            dma((2,)),
            dma((F,)),
            dma((S, F)),
            dma((F,)),
            dma((S, F)),
            dma((F,)),
            dma((S, F)),
            dma((F,)),
            dma((S, F)),
            dma((2,)),
        ],
        compiler_params=pltpu.CompilerParams(
            collective_id=0, has_side_effects=True, vmem_limit_bytes=52 << 20
        ),
        name="decode_steps",
    )(looked, gain, gub, gua_t, dbt, da, gate_base, up_base, down_base)


def on_device_kernels(
    x_chips, token_ids, embed_table, norm_gain, gate_base, up_base, down_base,
    gate_up_b, gate_up_a, down_b, down_a,
):
    F = lax.axis_size("fsdp")
    R = down_a.shape[0]
    looked = gather_columns(token_ids, embed_table)
    gain = norm_gain.astype(f32).reshape(F, -1)
    dbt = jnp.pad(down_b.T, ((0, R), (0, 0)))
    out = decode_steps(
        F, x_chips, looked, gain, gate_up_b, gate_up_a.T, dbt, down_a,
        gate_base, up_base, down_base,
    )
    return out.reshape(token_ids.shape[1], -1)


def on_device_plain(
    token_ids, embed_table, norm_gain, gate_base, up_base, down_base,
    gate_up_b, gate_up_a, down_b, down_a,
):
    tensor_slot = lax.axis_index("tensor")
    column_slot = lax.axis_index("fsdp") * lax.axis_size("tensor") + tensor_slot
    hidden_dev = gate_base.shape[0]
    columns_dev = embed_table.shape[0]
    rank_size = down_a.shape[0]
    model_width = gate_base.shape[1]
    rows_count = token_ids.shape[1]
    step_count = token_ids.shape[0]
    contract = (((0,), (1,)), ((), ()))
    narrow_local = lax.dynamic_slice_in_dim(gate_up_a, tensor_slot * hidden_dev, hidden_dev, 1)
    down_local = lax.dynamic_slice_in_dim(down_b, tensor_slot * hidden_dev, hidden_dev, 0)
    portion = lax.all_gather(gate_up_b, "fsdp", axis=0, tiled=True)
    gate_fix = lax.dot_general(
        narrow_local[:rank_size], portion[:, :rank_size], contract, preferred_element_type=f32
    )
    up_fix = lax.dot_general(
        narrow_local[rank_size:], portion[:, rank_size:], contract, preferred_element_type=f32
    )
    merged_inputs = jnp.concatenate(
        [
            (gate_base.astype(f32) + gate_fix).astype(bf16),
            (up_base.astype(f32) + up_fix).astype(bf16),
        ],
        axis=0,
    )
    down_fix = jnp.dot(
        down_local,
        lax.all_gather(down_a, "fsdp", axis=1, tiled=True),
        preferred_element_type=f32,
    )
    merged_down = (down_base.astype(f32) + down_fix).astype(bf16)
    looked_local = jnp.transpose(jnp.take(embed_table, token_ids, axis=1), (1, 2, 0))
    looked = lax.all_gather(looked_local, ("fsdp", "tensor"), axis=2, tiled=True)
    gain_value = norm_gain.astype(f32)
    stream = jnp.zeros((rows_count, model_width), f32)
    for position in range(step_count):
        stream = stream + looked[position].astype(f32)
        inverse_rms = lax.rsqrt(jnp.mean(stream * stream, axis=1, keepdims=True) + epsilon)
        normed = (stream * inverse_rms * gain_value).astype(bf16)
        preact = lax.dot_general(normed, merged_inputs, NT, preferred_element_type=f32)
        activated = (jax.nn.silu(preact[:, :hidden_dev]) * preact[:, hidden_dev:]).astype(bf16)
        stream = stream + lax.psum(
            jnp.dot(activated, merged_down, preferred_element_type=f32), ("fsdp", "tensor")
        )
    result = lax.dynamic_slice_in_dim(stream, column_slot * columns_dev, columns_dev, 1)
    return result.astype(bf16)


def solution(mesh):
    in_specs = (
        P(None, "groups"),
        P(("fsdp", "tensor"), None),
        P(),
        P(("fsdp", "tensor"), None),
        P(("fsdp", "tensor"), None),
        P(("fsdp", "tensor"), None),
        P("fsdp", None),
        P(None, "fsdp"),
        P("fsdp", None),
        P(None, "fsdp"),
    )
    out_specs = P("groups", ("fsdp", "tensor"))
    fits = mesh.shape["fsdp"] == 8 and mesh.shape["tensor"] == 2
    body = functools.partial(on_device_kernels, 2) if fits else on_device_plain
    return jax.shard_map(
        body, mesh=mesh, in_specs=in_specs, out_specs=out_specs, check_vma=False
    )
```

```python
import functools
import jax
import jax.numpy as jnp
from jax import lax
from jax.experimental import pallas as pl
from jax.experimental.pallas import tpu as pltpu
from jax.sharding import PartitionSpec as P

epsilon = 1e-06
bf16, f32 = jnp.bfloat16, jnp.float32
NT = (((1,), (1,)), ((), ()))
MESH = pl.DeviceIdType.MESH


def gather_kernel(ids_ref, table_ref, out_ref, blocks, placed, sems):
    count = blocks.shape[0]
    rows = table_ref.shape[0]

    def block_copy(i):
        start = pl.multiple_of((ids_ref[i] // 128) * 128, 128)
        return pltpu.make_async_copy(
            table_ref.at[:, pl.ds(start, 128)], blocks.at[i], sems.at[i]
        )

    unroll = 8

    def begin(i, carry):
        for u in range(unroll):
            block_copy(i * unroll + u).start()
        return carry

    lax.fori_loop(0, count // unroll, begin, 0)
    placed[...] = jnp.zeros_like(placed)
    group = 64
    lane = lax.broadcasted_iota(jnp.int32, (group, 128), 1)

    def place(i, carry):
        for u in range(unroll):
            block_copy(i * unroll + u).wait()
        for r in range(0, rows, group):
            kept = placed[r:r + group, :]
            for u in range(unroll):
                token = i * unroll + u
                shift = lax.rem(token + 128 - lax.rem(ids_ref[token], 128), 128)
                turned = pltpu.roll(blocks[token, r:r + group].astype(f32), shift, 1)
                kept = jnp.where(lane == token, turned, kept)
            placed[r:r + group, :] = kept
        return carry

    lax.fori_loop(0, count // unroll, place, 0)
    out = jnp.transpose(placed[...])[:, :rows].astype(bf16)
    out_ref[...] = out.reshape(out_ref.shape)


def gather_columns(token_ids, table):
    steps, rows = token_ids.shape
    count = steps * rows
    width = table.shape[0]
    padded = (width + 127) // 128 * 128
    return pl.pallas_call(
        gather_kernel,
        out_shape=jax.ShapeDtypeStruct((steps, 2, rows // 2, width), bf16),
        in_specs=[
            pl.BlockSpec(memory_space=pltpu.SMEM),
            pl.BlockSpec(memory_space=pl.ANY),
        ],
        out_specs=pl.BlockSpec(memory_space=pltpu.VMEM),
        scratch_shapes=[
            pltpu.VMEM((count, width, 128), bf16),
            pltpu.VMEM((padded, 128), f32),
            pltpu.SemaphoreType.DMA((count,)),
        ],
        compiler_params=pltpu.CompilerParams(vmem_limit_bytes=24 << 20),
        cost_estimate=pl.CostEstimate(
            flops=count * width * 128, bytes_accessed=count * width * 256, transcendentals=0
        ),
        name="embed_columns",
    )(token_ids.reshape(count), table)


def decode_kernel(
    F, X, looked_ref, gain_ref, gub_ref, gua_ref, dbt_ref, da_ref, gate_hbm, up_hbm, down_hbm,
    out_ref,
    wg, wu, wd, db, ag, stream, added, looked_in, acc_g, acc_u, act,
    sib_out, sib_in, own_part, rs_out, rs_in, fin_out, fin_in,
    w_sem, look_sem, ag_send, ag_recv, fw_send, fw_recv, sib_send, sib_recv, rs_send, rs_recv,
    fin_sem,
):
    S = looked_ref.shape[0]
    H = wg.shape[1]
    C = wg.shape[2]
    half = C // 2
    R = da_ref.shape[0]
    rows = 32
    Z = F // X
    grp = lax.axis_index("groups")
    me = lax.axis_index("fsdp")
    t = lax.axis_index("tensor")
    other = 1 - t
    z, x = me // X, me % X

    def ahead(k):
        return ((z + k // X) % Z) * X + (x + k % X) % X

    def behind(k):
        return ((z + Z - k // X) % Z) * X + (x + X - k % X) % X

    def w_copies(j, i):
        cols = pl.ds(pl.multiple_of(j * C, 128), C)
        return [
            pltpu.make_async_copy(h.at[:, cols], w.at[j], w_sem.at[n, i])
            for n, (h, w) in enumerate(((gate_hbm, wg), (up_hbm, wu), (down_hbm, wd)))
        ]

    for k in range(F):
        for c in w_copies(behind(k), k)[:2]:
            c.start()
    for i, k in enumerate(list(range(1, F)) + [0]):
        w_copies(ahead(k), i)[2].start()

    barrier = pltpu.get_barrier_semaphore()
    for k in range(1, F):
        pl.semaphore_signal(barrier, inc=1, device_id=(grp, ahead(k), t), device_id_type=MESH)
    pl.semaphore_signal(barrier, inc=1, device_id=(grp, me, other), device_id_type=MESH)
    pl.semaphore_wait(barrier, F)

    def remote(src, dst, ss, rs, dev):
        return pltpu.make_async_remote_copy(
            src_ref=src, dst_ref=dst, send_sem=ss, recv_sem=rs, device_id=dev, device_id_type=MESH
        )

    sibling = (grp, me, other)
    look = remote(looked_ref.at[:, other], looked_in, look_sem.at[0], look_sem.at[1], sibling)
    look.start()
    wide = dbt_ref[...]
    db[...] = jnp.where(t == 0, wide[:, :H].astype(f32), wide[:, H:].astype(f32)).astype(bf16)
    mine = looked_ref[:, t].astype(f32)
    look.wait()
    theirs = looked_in[...].astype(f32)
    for s in range(S):
        left = jnp.where(t == 0, mine[s], theirs[s])
        right = jnp.where(t == 0, theirs[s], mine[s])
        added[s] = jnp.concatenate([left, right], axis=1)
    stream[...] = jnp.zeros_like(stream)
    lane = lax.broadcasted_iota(jnp.int32, (rows, 2 * R), 1)

    def step(s, carry):
        now = stream[...] + added[s]
        stream[...] = now
        scaled = (now * gain_ref[pl.ds(me, 1), :]).astype(bf16)
        low = jnp.dot(scaled, gub_ref[...], preferred_element_type=f32)
        ag[s, me, t, :, :C] = now.astype(bf16)
        ag[s, me, t, :, C:] = low.astype(bf16)

        def ag_copy(j_from, k, dev):
            piece = ag.at[s, j_from, t]
            return remote(piece, piece, ag_send.at[k], ag_recv.at[s, j_from], dev)

        def fw_copy(j_from, k):
            piece = ag.at[s, j_from, t]
            return remote(piece, piece, fw_send.at[k], fw_recv.at[s, j_from], sibling)

        fw_copy(me, 0).start()
        for k in range(1, F):
            ag_copy(me, k, (grp, ahead(k), t)).start()

        squares = jnp.zeros((rows, 1), f32)
        lows = jnp.zeros((rows, 2 * R), f32)
        for k in range(F):
            if k + 1 < F:
                j_next = behind(k + 1)
                ag_copy(j_next, k + 1, (grp, j_next, t)).wait_recv()
                fw_copy(j_next, k + 1).start()
            j = behind(k)
            theirs_in = ag.at[s, j, other]
            remote(
                theirs_in, theirs_in, fw_send.at[k], fw_recv.at[s, j], sibling
            ).wait_recv()

            @pl.when(s == 0)
            def _():
                for c in w_copies(j, k)[:2]:
                    c.wait()

            piece = ag[s, j].reshape(rows, C + 2 * R)
            xs = piece[:, :C].astype(f32)
            squares += jnp.sum(xs * xs, axis=1, keepdims=True)
            lows += piece[:, C:].astype(f32)
            xn = (xs * gain_ref[pl.ds(j, 1), :]).astype(bf16)
            g = lax.dot_general(xn, wg[j], NT, preferred_element_type=f32)
            u = lax.dot_general(xn, wu[j], NT, preferred_element_type=f32)
            if k == 0:
                acc_g[...] = g
                acc_u[...] = u
            else:
                acc_g[...] += g
                acc_u[...] += u
        for k in range(1, F):
            ag_copy(me, k, (grp, ahead(k), t)).wait_send()
        for k in range(F):
            fw_copy(behind(k), k).wait_send()

        inverse_rms = lax.rsqrt(squares / (F * C) + epsilon)
        a_local = gua_ref[pl.ds(pl.multiple_of(t * H, 16), H), :]
        zero = jnp.zeros_like(lows)
        low_g = jnp.where(lane < R, lows, zero).astype(bf16)
        low_u = jnp.where(lane < R, zero, lows).astype(bf16)
        gate = acc_g[...] + lax.dot_general(low_g, a_local, NT, preferred_element_type=f32)
        up = acc_u[...] + lax.dot_general(low_u, a_local, NT, preferred_element_type=f32)
        gate = gate * inverse_rms
        up = up * inverse_rms
        act[...] = (gate / (1.0 + jnp.exp(-gate)) * up).astype(bf16)

        down_low = lax.dot_general(act[...], db[...], NT, preferred_element_type=f32)
        low_mine = jnp.where(t == 0, down_low[:16], down_low[16:])
        low_other = jnp.where(t == 0, down_low[16:], down_low[:16]).astype(bf16)

        def sib_copy(j):
            return remote(
                sib_out.at[j], sib_in.at[s, j], sib_send.at[j], sib_recv.at[s, j], sibling
            )

        def rs_copy(k):
            j = ahead(k)
            return remote(
                rs_out.at[j], rs_in.at[s, me], rs_send.at[k], rs_recv.at[s, me], (grp, j, t)
            )

        def finish(k):
            j = ahead(k)
            sib_copy(j).wait_recv()
            total = own_part[j] + sib_in[s, j].astype(f32)
            if k > 0:
                rs_out[j] = total.astype(bf16)
                rs_copy(k).start()
            return total

        order = list(range(1, F)) + [0]
        total = None
        for i, k in enumerate(order):
            j = ahead(k)

            @pl.when(s == 0)
            def _():
                w_copies(j, i)[2].wait()

            part = jnp.dot(act[...], wd[j], preferred_element_type=f32)
            own_part[j, :, :C] = jnp.where(t == 0, part[:16], part[16:])
            own_part[j, :, C:] = low_mine
            sib_out[j, :, :C] = jnp.where(t == 0, part[16:], part[:16]).astype(bf16)
            sib_out[j, :, C:] = low_other
            sib_copy(j).start()
            if i > 0:
                finish(order[i - 1])
        total = finish(0)
        for k in range(1, F):
            j = behind(k)
            remote(
                rs_out.at[j], rs_in.at[s, j], rs_send.at[k], rs_recv.at[s, j], (grp, j, t)
            ).wait_recv()
            total += rs_in[s, j].astype(f32)
        fix = jnp.dot(total[:, C:C + R].astype(bf16), da_ref[...], preferred_element_type=f32)
        stream[...] = stream[...] + total[:, :C] + fix
        for k in range(F):
            sib_copy(ahead(k)).wait_send()
            if k > 0:
                rs_copy(k).wait_send()
        return carry

    lax.fori_loop(0, S, step, 0)

    last = stream[...]
    keep = jnp.where(t == 0, last[:, :half], last[:, half:])
    fin_out[...] = jnp.where(t == 0, last[:, half:], last[:, :half]).astype(bf16)
    fin = remote(fin_out, fin_in, fin_sem.at[0], fin_sem.at[1], sibling)
    fin.start()
    out_ref[t] = keep.astype(bf16)
    fin.wait()
    out_ref[other] = fin_in[...]


def decode_steps(F, X, looked, gain, gub, gua_t, dbt, da, gate_base, up_base, down_base):
    S = looked.shape[0]
    H, D = gate_base.shape
    C = D // F
    R = da.shape[0]
    W = C + 2 * R
    vmem = pl.BlockSpec(memory_space=pltpu.VMEM)
    hbm = pl.BlockSpec(memory_space=pl.ANY)
    dma = pltpu.SemaphoreType.DMA
    return pl.pallas_call(
        functools.partial(decode_kernel, F, X),
        out_shape=jax.ShapeDtypeStruct((2, 16, C // 2), bf16),
        in_specs=[vmem] * 6 + [hbm] * 3,
        out_specs=vmem,
        scratch_shapes=[
            pltpu.VMEM((F, H, C), bf16),
            pltpu.VMEM((F, H, C), bf16),
            pltpu.VMEM((F, H, C), bf16),
            pltpu.VMEM((2 * R, H), bf16),
            pltpu.VMEM((S, F, 2, 16, W), bf16),
            pltpu.VMEM((16, C), f32),
            pltpu.VMEM((S, 16, C), f32),
            pltpu.VMEM((S, 16, C // 2), bf16),
            pltpu.VMEM((32, H), f32),
            pltpu.VMEM((32, H), f32),
            pltpu.VMEM((32, H), bf16),
            pltpu.VMEM((F, 16, W), bf16),
            pltpu.VMEM((S, F, 16, W), bf16),
            pltpu.VMEM((F, 16, W), f32),
            pltpu.VMEM((F, 16, W), bf16),
            pltpu.VMEM((S, F, 16, W), bf16),
            pltpu.VMEM((16, C // 2), bf16),
            pltpu.VMEM((16, C // 2), bf16),
            dma((3, F)),
            dma((2,)),
            dma((F,)),
            dma((S, F)),
            dma((F,)),
            dma((S, F)),
            dma((F,)),
            dma((S, F)),
            dma((F,)),
            dma((S, F)),
            dma((2,)),
        ],
        compiler_params=pltpu.CompilerParams(
            collective_id=0, has_side_effects=True, vmem_limit_bytes=52 << 20
        ),
        name="decode_steps",
    )(looked, gain, gub, gua_t, dbt, da, gate_base, up_base, down_base)


def on_device_kernels(
    x_chips, token_ids, embed_table, norm_gain, gate_base, up_base, down_base,
    gate_up_b, gate_up_a, down_b, down_a,
):
    F = lax.axis_size("fsdp")
    R = down_a.shape[0]
    looked = gather_columns(token_ids, embed_table)
    gain = norm_gain.astype(f32).reshape(F, -1)
    dbt = jnp.pad(down_b.T, ((0, R), (0, 0)))
    out = decode_steps(
        F, x_chips, looked, gain, gate_up_b, gate_up_a.T, dbt, down_a,
        gate_base, up_base, down_base,
    )
    return out.reshape(token_ids.shape[1], -1)


def on_device_plain(
    token_ids, embed_table, norm_gain, gate_base, up_base, down_base,
    gate_up_b, gate_up_a, down_b, down_a,
):
    tensor_slot = lax.axis_index("tensor")
    column_slot = lax.axis_index("fsdp") * lax.axis_size("tensor") + tensor_slot
    hidden_dev = gate_base.shape[0]
    columns_dev = embed_table.shape[0]
    rank_size = down_a.shape[0]
    model_width = gate_base.shape[1]
    rows_count = token_ids.shape[1]
    step_count = token_ids.shape[0]
    contract = (((0,), (1,)), ((), ()))
    narrow_local = lax.dynamic_slice_in_dim(gate_up_a, tensor_slot * hidden_dev, hidden_dev, 1)
    down_local = lax.dynamic_slice_in_dim(down_b, tensor_slot * hidden_dev, hidden_dev, 0)
    portion = lax.all_gather(gate_up_b, "fsdp", axis=0, tiled=True)
    gate_fix = lax.dot_general(
        narrow_local[:rank_size], portion[:, :rank_size], contract, preferred_element_type=f32
    )
    up_fix = lax.dot_general(
        narrow_local[rank_size:], portion[:, rank_size:], contract, preferred_element_type=f32
    )
    merged_inputs = jnp.concatenate(
        [
            (gate_base.astype(f32) + gate_fix).astype(bf16),
            (up_base.astype(f32) + up_fix).astype(bf16),
        ],
        axis=0,
    )
    down_fix = jnp.dot(
        down_local,
        lax.all_gather(down_a, "fsdp", axis=1, tiled=True),
        preferred_element_type=f32,
    )
    merged_down = (down_base.astype(f32) + down_fix).astype(bf16)
    looked_local = jnp.transpose(jnp.take(embed_table, token_ids, axis=1), (1, 2, 0))
    looked = lax.all_gather(looked_local, ("fsdp", "tensor"), axis=2, tiled=True)
    gain_value = norm_gain.astype(f32)
    stream = jnp.zeros((rows_count, model_width), f32)
    for position in range(step_count):
        stream = stream + looked[position].astype(f32)
        inverse_rms = lax.rsqrt(jnp.mean(stream * stream, axis=1, keepdims=True) + epsilon)
        normed = (stream * inverse_rms * gain_value).astype(bf16)
        preact = lax.dot_general(normed, merged_inputs, NT, preferred_element_type=f32)
        activated = (jax.nn.silu(preact[:, :hidden_dev]) * preact[:, hidden_dev:]).astype(bf16)
        stream = stream + lax.psum(
            jnp.dot(activated, merged_down, preferred_element_type=f32), ("fsdp", "tensor")
        )
    result = lax.dynamic_slice_in_dim(stream, column_slot * columns_dev, columns_dev, 1)
    return result.astype(bf16)


def solution(mesh):
    in_specs = (
        P(None, "groups"),
        P(("fsdp", "tensor"), None),
        P(),
        P(("fsdp", "tensor"), None),
        P(("fsdp", "tensor"), None),
        P(("fsdp", "tensor"), None),
        P("fsdp", None),
        P(None, "fsdp"),
        P("fsdp", None),
        P(None, "fsdp"),
    )
    out_specs = P("groups", ("fsdp", "tensor"))
    fits = mesh.shape["fsdp"] == 8 and mesh.shape["tensor"] == 2
    body = functools.partial(on_device_kernels, 2) if fits else on_device_plain
    return jax.shard_map(
        body, mesh=mesh, in_specs=in_specs, out_specs=out_specs, check_vma=False
    )
```
